32 devices in a mesh: atoms: 16 (over z, x, core), waves: 2 (over y).
Axes of the slice: x: 2, y: 2, z: 4, core: 2. Of those that a mesh axis runs over, the one named last changes fastest.
Arguments:
- features: bfloat16 [64, 32768], P(None, 'atoms'), may hold values from -6 to 6
- coords: float32 [3, 32768], P(None, 'atoms'), may hold values from 0 to 1
- neighbours: int32 [27, 256], P(None, 'atoms'), may hold values from 0 to 255, as said below
- live_slots: int32 [27, 256], P(None, 'atoms'), may hold values 0 or 1
- block_count: int32 [16], P('atoms'), may hold values from 8 to 16, as said below
- kvec: int32 [3, 4096], P(None, 'waves'), may hold values from -32 to 32, as said below
- msg_weight: bfloat16 [1, 64, 64], replicated, may hold values from -0.75 to 0.75
- filter_weight: float32 [1, 64, 64], replicated, may hold values from -0.75 to 0.75
- mlp_in: bfloat16 [1, 128, 192], replicated, may hold values from -0.4375 to 0.4375
- mlp_out: bfloat16 [1, 64, 128], replicated, may hold values from -0.5 to 0.5
Outputs:
- updated: bfloat16 [64, 32768], P(None, 'atoms')
The draws below stay inside these ranges and needn't reach their ends.
Inputs may be any that keep to these rules, and one draw needn't show every extreme that they name: `neighbours`: entry [s, b] names a block slot whose index of atoms, slot // 16, equals b // 16 or lies one before or one after it, cyclically, and which is live. `block_count`: some index of atoms has all 16 of its slots live in every draw. `kvec`: rows 1 and 2 lie in -5 to 5; no column is zero in all three rows.
All inputs are finite; a program needn't handle non-finite values. No bound on the sum of `live_slots` on one device may be relied on, other than what follows from the above.
Results may differ from the reference program's by a relative error of at most 0.0062.
Values may be sent and summed in bfloat16 or wider, within the bound.
A program may use at most 64 MiB of HBM per device.

```python
import math
import jax
import jax.numpy as jnp
from jax import lax

C = 64
K = 4096
HID = 128
BLOCK = 128
SLOTS = 27
LAYERS = 1
BCAP = 16
NBLOCKS = 256
NATOMS = 32768
N_ATOMS = 16


def counts_of(key):
    first, second = jax.random.split(jax.random.fold_in(key, 11))
    counts = jax.random.randint(first, (N_ATOMS,), BCAP // 2, BCAP + 1)
    fullest = jax.random.randint(second, (), 0, N_ATOMS)
    return jnp.where(jnp.arange(N_ATOMS) == fullest, BCAP, counts).astype(jnp.int32)


def draw_block_count(key, part):
    return counts_of(key)


def draw_neighbours(key, part):
    counts = counts_of(key)
    first, second = jax.random.split(jax.random.fold_in(key, 23))
    home = jnp.arange(N_ATOMS * BCAP, dtype=jnp.int32) // BCAP
    step = jax.random.randint(first, (SLOTS, N_ATOMS * BCAP), -1, 2)
    source = (home[None, :] + step) % N_ATOMS
    local = jax.random.randint(second, (SLOTS, N_ATOMS * BCAP), 0, counts[source])
    return (source * BCAP + local).astype(jnp.int32)


def draw_kvec(key, part):
    first, second, third = jax.random.split(jax.random.fold_in(key, 37), 3)
    along = jax.random.randint(first, (K,), -2 * N_ATOMS, 2 * N_ATOMS + 1)
    across = jax.random.randint(second, (K,), -5, 6)
    upward = jax.random.randint(third, (K,), -5, 6)
    zero = (along == 0) & (across == 0) & (upward == 0)
    upward = jnp.where(zero, 1, upward)
    return jnp.stack([along, across, upward]).astype(jnp.int32)


def draw_coords(key, part):
    total = N_ATOMS * BCAP * BLOCK
    unit = jax.random.uniform(jax.random.fold_in(key, 41), (3, total), jnp.float32)
    region = (jnp.arange(total) // (BCAP * BLOCK)).astype(jnp.float32)
    along = jnp.mod((region - 0.5 + 2.0 * unit[0]) / N_ATOMS, 1.0)
    along = jnp.minimum(along, 0.9999)
    return jnp.stack([along, unit[1], unit[2]]).astype(jnp.float32)


def place_ends(array, key, least, largest):
    longest = array.shape.index(max(array.shape))
    spots = []
    for shift in (0, 1):
        where = [jax.random.randint(jax.random.fold_in(key, axis), (), 0, length) for axis, length in enumerate(array.shape)]
        where[longest] = (where[longest] + shift) % array.shape[longest]
        spots.append(tuple(where))
    return array.at[spots[0]].set(least).at[spots[1]].set(largest)


def block_scale(own_key, extent, cuts, least, high):
    level = 1.0
    for dim, parts in cuts:
        steps = jax.random.uniform(jax.random.fold_in(jax.random.fold_in(own_key, 6), dim), (parts,), jnp.float32, least / len(cuts), high / len(cuts))
        level = level * jnp.repeat(jnp.exp(steps), extent[dim] // parts).reshape((-1,) + (1,) * (len(extent) - 1 - dim))
    return level


def normal_values(key, shape, scale, most, cuts=(), kind=jnp.bfloat16):
    array = scale * jax.random.normal(key, shape, jnp.float32)
    if cuts:
        array = array * block_scale(key, shape, cuts, -0.22, 0.18)
    return jnp.clip(array, -most, most).astype(kind)


def setup_inputs(seed: int = 0) -> dict:
    splits = jax.random.split(jax.random.key(seed), 11)
    features = normal_values(splits[0], (C, NATOMS), 1.0, 6.0, ((1, 16),))
    coords = draw_coords(jax.random.fold_in(splits[10], 71), 0)
    neighbours = draw_neighbours(jax.random.fold_in(splits[10], 71), 0)
    live_slots = place_ends((jax.random.randint(splits[3], (SLOTS, NBLOCKS), 0, 5) < 4).astype(jnp.int32), jax.random.fold_in(splits[3], 1), 0, 1)
    block_count = draw_block_count(jax.random.fold_in(splits[10], 71), 0)
    kvec = draw_kvec(jax.random.fold_in(splits[10], 71), 0)
    msg_weight = normal_values(splits[6], (LAYERS, C, C), C ** -0.5, 0.75)
    filter_weight = normal_values(splits[7], (LAYERS, C, C), C ** -0.5, 0.75, (), jnp.float32)
    mlp_in = normal_values(splits[8], (LAYERS, HID, 3 * C), (3 * C) ** -0.5, 0.4375)
    mlp_out = normal_values(splits[9], (LAYERS, C, HID), HID ** -0.5, 0.5)
    return dict(features=features, coords=coords, neighbours=neighbours, live_slots=live_slots, block_count=block_count, kvec=kvec, msg_weight=msg_weight, filter_weight=filter_weight, mlp_in=mlp_in, mlp_out=mlp_out)


TWO_PI = 6.283185307179586
MSG_SCALE = 0.125
GAIN_TOP = 20.0

def pair_weights(own, near, scale_x, live):
    total = None
    for axis in range(3):
        diff = own[axis][None, :, :, None] - near[axis][:, :, None, :]
        diff = diff - jnp.floor(diff + 0.5)
        if axis == 0:
            diff = diff * scale_x
        total = diff * diff if total is None else total + diff * diff
    return (jnp.exp(-2.0 * total) * live[:, :, None, None]).astype(jnp.bfloat16)

def phase_tables(kf_rows, coords_group):
    theta = TWO_PI * (kf_rows[0][:, None] * coords_group[0][None, :] + kf_rows[1][:, None] * coords_group[1][None, :] + kf_rows[2][:, None] * coords_group[2][None, :])
    return (jnp.cos(theta).astype(jnp.bfloat16), jnp.sin(theta).astype(jnp.bfloat16))

def short_range(hm, coords, neighbours, live_slots):
    chans = hm.shape[0]
    nbl = neighbours.shape[1]
    hm3 = hm.reshape(chans, nbl, BLOCK)
    pos3 = coords.reshape(3, nbl, BLOCK)

    def group(index):
        blocks = index * 2 + jnp.arange(2, dtype=jnp.int32)
        idx = neighbours[:, blocks]
        live = live_slots[:, blocks].astype(jnp.float32)
        weights = pair_weights(pos3[:, blocks], pos3[:, idx], N_ATOMS, live)
        near = hm3[:, idx]
        msg = jnp.einsum('csbj,sbij->cbi', near.astype(jnp.float32), weights.astype(jnp.float32))
        return (msg * MSG_SCALE).astype(jnp.bfloat16)
    out = lax.map(group, jnp.arange(nbl // 2, dtype=jnp.int32))
    return out.transpose(1, 0, 2, 3).reshape(chans, nbl * BLOCK)

def structure(kf, coords, masked):
    size = 4 * BLOCK
    groups = masked.shape[1] // size
    chans = masked.shape[0]
    dims = (((1,), (1,)), ((), ()))

    def step(acc, index):
        start = index * size
        pos = lax.dynamic_slice_in_dim(coords, start, size, 1)
        part = lax.dynamic_slice_in_dim(masked, start, size, 1)
        cosb, sinb = phase_tables(kf, pos)
        term = jnp.concatenate([lax.dot_general(cosb, part, dims, preferred_element_type=jnp.float32), lax.dot_general(sinb, part, dims, preferred_element_type=jnp.float32)], axis=1)
        return (acc + term, None)
    acc, _ = lax.scan(step, jnp.zeros((kf.shape[1], 2 * chans), jnp.float32), jnp.arange(groups, dtype=jnp.int32))
    return acc

def spectral(factor, gain, mixing, total):
    chans = mixing.shape[0]
    scaled = factor * (1.0 / math.sqrt(total))
    cos_part = jnp.dot(scaled[:, :chans], mixing, precision=lax.Precision.HIGHEST)
    sin_part = jnp.dot(scaled[:, chans:], mixing, precision=lax.Precision.HIGHEST)
    return (jnp.concatenate([cos_part, sin_part], axis=1) * gain[:, None]).astype(jnp.bfloat16)

def potentials(filtered, kf, coords):
    size = 4 * BLOCK
    chans = filtered.shape[1] // 2
    groups = coords.shape[1] // size
    dims = (((0,), (0,)), ((), ()))

    def step(carry, index):
        pos = lax.dynamic_slice_in_dim(coords, index * size, size, 1)
        cosb, sinb = phase_tables(kf, pos)
        term = lax.dot_general(filtered[:, :chans], cosb, dims, preferred_element_type=jnp.float32) + lax.dot_general(filtered[:, chans:], sinb, dims, preferred_element_type=jnp.float32)
        return (carry, term * (1.0 / math.sqrt(K)))
    _, out = lax.scan(step, 0, jnp.arange(groups, dtype=jnp.int32))
    return out.transpose(1, 0, 2).reshape(chans, groups * size)

def update(h, msg, potential, live, first_layer, second_layer):
    stacked = jnp.concatenate([h, msg, potential.astype(jnp.bfloat16)], axis=0)
    hidden = jax.nn.silu(jnp.dot(first_layer, stacked, preferred_element_type=jnp.float32)).astype(jnp.bfloat16)
    out = h.astype(jnp.float32) + jnp.dot(second_layer, hidden, preferred_element_type=jnp.float32)
    return jnp.where(live[None, :], out, jnp.zeros_like(out)).astype(jnp.bfloat16)

def reference(features, coords, neighbours, live_slots, block_count, kvec, msg_weight, filter_weight, mlp_in, mlp_out):
    nbl = BCAP * N_ATOMS
    total = nbl * BLOCK
    slot = jnp.arange(nbl, dtype=jnp.int32)
    live_block = slot % BCAP < block_count[slot // BCAP]
    live = jnp.repeat(live_block, BLOCK)
    kf = kvec.astype(jnp.float32)
    kx = kf[0] / N_ATOMS
    gain = GAIN_TOP / (4.0 + kx * kx + kf[1] * kf[1] + kf[2] * kf[2])
    h = features
    for layer in range(LAYERS):
        hm = jnp.dot(msg_weight[layer], h, preferred_element_type=jnp.float32).astype(jnp.bfloat16)
        msg = short_range(hm, coords, neighbours, live_slots)
        masked = jnp.where(live[None, :], h, jnp.zeros_like(h))
        factor = structure(kf, coords, masked)
        filtered = spectral(factor, gain, filter_weight[layer], total)
        potential = potentials(filtered, kf, coords)
        h = update(h, msg, potential, live, mlp_in[layer], mlp_out[layer])
    return h
```

```python
import functools
import math

import jax
import jax.numpy as jnp
from jax import lax
from jax.experimental import pallas as pl
from jax.experimental.pallas import tpu as pltpu
from jax.sharding import PartitionSpec as P

BLOCK = 128
MSG_SCALE = 0.125
GAIN_TOP = 20.0
SIDE = 5
BASE = 2 * SIDE + 1
HALF = (BASE * BASE + 1) // 2
BATCH = 4
F32 = jnp.float32
BF16 = jnp.bfloat16
VMEM = pl.BlockSpec(memory_space=pltpu.VMEM)
SMEM = pl.BlockSpec(memory_space=pltpu.SMEM)
NT = (((1,), (1,)), ((), ()))
TN = (((0,), (0,)), ((), ()))
PARAMS = pltpu.CompilerParams(vmem_limit_bytes=48 * 1024 * 1024)


def phase_rows(ta, tb_ref, pair, held):
    half = tb_ref.shape[0] // 2
    cb = tb_ref[pl.ds(pair, 1), :].astype(BF16)
    sb = tb_ref[pl.ds(half + pair, 1), :].astype(BF16)
    return ta * cb, ta * sb


def groups_of(count):
    return [(i, min(4, count - i)) for i in range(0, count, 4)]


def structure_kernel(pairs, ta_ref, tb_ref, h_ref, out_ref):
    a = ta_ref.shape[0]
    out_ref[...] = jnp.zeros_like(out_ref)
    ta = ta_ref[...]
    h = h_ref[...]
    for first, size in groups_of(pairs):
        cs, ss = zip(*[phase_rows(ta, tb_ref, first + i, pairs) for i in range(size)])
        rows = slice(first * a, (first + size) * a)
        out_ref[rows, 0:64] = lax.dot_general(jnp.concatenate(cs, 0), h, NT, preferred_element_type=F32)
        out_ref[rows, 64:128] = lax.dot_general(jnp.concatenate(ss, 0), h, NT, preferred_element_type=F32)
    rows = tb_ref.shape[0]
    out_ref[pairs * a : pairs * a + rows, 0:64] = lax.dot_general(
        tb_ref[...].astype(BF16), h, NT, preferred_element_type=F32
    )


def potentials_kernel(pairs, scale, ta_ref, tb_ref, g_ref, out_ref):
    a = ta_ref.shape[0]
    ta = ta_ref[...]
    rows = tb_ref.shape[0]
    acc = lax.dot_general(
        g_ref[pairs * a : pairs * a + rows, 0:64], tb_ref[...].astype(BF16), TN, preferred_element_type=F32
    )
    for first, size in groups_of(pairs):
        cs, ss = zip(*[phase_rows(ta, tb_ref, first + i, pairs) for i in range(size)])
        g = g_ref[first * a : (first + size) * a, :]
        acc += lax.dot_general(g[:, 0:64], jnp.concatenate(cs, 0), TN, preferred_element_type=F32)
        acc += lax.dot_general(g[:, 64:128], jnp.concatenate(ss, 0), TN, preferred_element_type=F32)
    out_ref[...] = (acc * scale).astype(BF16)


def short_kernel(scale_x, idx_ref, live_ref, own_ref, near_ref, hm_ref, out_ref):
    blocks = own_ref.shape[0]
    steps = idx_ref.shape[0] // BATCH

    def block_step(b, _):
        own = own_ref[b]
        cols = [jnp.broadcast_to(own[:, d : d + 1], (BLOCK, BLOCK)) for d in range(3)]

        def slot_step(step, acc):
            weights, mapped = [], []
            for u in range(BATCH):
                s = step * BATCH + u
                n = idx_ref[s, b]
                near = near_ref[n]
                total = None
                for d in (1, 2, 0):
                    diff = cols[d] - near[d : d + 1, :]
                    diff = diff - jnp.round(diff)
                    if d == 0:
                        diff = diff * scale_x
                    total = diff * diff if total is None else total + diff * diff
                weights.append(jnp.exp(-2.0 * total).astype(BF16))
                mapped.append(hm_ref[n] * live_ref[s, b].astype(BF16))
            return acc + lax.dot_general(
                jnp.concatenate(mapped, 1), jnp.concatenate(weights, 1), NT, preferred_element_type=F32
            )

        acc = lax.fori_loop(0, steps, slot_step, jnp.zeros((hm_ref.shape[1], BLOCK), F32))
        out_ref[b] = (acc * MSG_SCALE).astype(BF16)
        return 0

    lax.fori_loop(0, blocks, block_step, 0)


def update_kernel(count_ref, h_ref, msg_ref, pot_ref, first_ref, second_ref, out_ref):
    h = h_ref[...]
    pot = pot_ref[0].astype(F32)
    for w in range(1, pot_ref.shape[0]):
        pot = pot + pot_ref[w].astype(F32)
    msg = jnp.concatenate([msg_ref[b] for b in range(msg_ref.shape[0])], 1)
    z = jnp.concatenate([h, msg, pot.astype(BF16)], 0)
    hidden = jnp.dot(first_ref[...], z, preferred_element_type=F32)
    hidden = (hidden * jax.nn.sigmoid(hidden)).astype(BF16)
    out = h.astype(F32) + jnp.dot(second_ref[...], hidden, preferred_element_type=F32)
    atom = lax.broadcasted_iota(jnp.int32, out.shape, 1)
    out_ref[...] = jnp.where(atom < count_ref[0] * BLOCK, out, 0.0).astype(BF16)


def call(kernel, shape, dtype, specs, *args):
    return pl.pallas_call(
        kernel,
        out_shape=jax.ShapeDtypeStruct(shape, dtype),
        in_specs=specs,
        out_specs=VMEM,
        compiler_params=PARAMS,
    )(*args)


def coefficients(kvec, regions, pairs, padded, first):
    top = 2 * regions
    k = jnp.where(kvec[0:1] < 0, -kvec, kvec)
    code = k[1] * BASE + k[2]
    n = jnp.abs(code) - first
    onehot_a = (jnp.arange(top + 1, dtype=F32)[:, None] == k[0][None, :]).astype(BF16)
    which = jnp.arange(pairs, dtype=F32)[:, None] == n[None, :]
    up = (which & (code >= 0)[None, :]).astype(BF16)
    down = (which & (code < 0)[None, :]).astype(BF16)
    m1 = lax.dot_general(up, onehot_a, NT, preferred_element_type=F32)
    m2 = lax.dot_general(down, onehot_a, NT, preferred_element_type=F32)
    b = jnp.arange(pairs, dtype=F32) + first
    ky = jnp.floor((b + SIDE) / BASE)
    kz = b - ky * BASE
    kx = jnp.arange(top + 1, dtype=F32) / regions
    gain = GAIN_TOP / (4.0 + (kx * kx)[None, :] + (ky * ky + kz * kz)[:, None])
    p = gain * (m1 + m2)
    q = gain * (m2 - m1)
    main_p, main_q = p[:, 1:], q[:, 1:]
    a = 2 * top
    p_rows = jnp.concatenate([main_p, main_p], 1).reshape(-1)
    q_cos = jnp.concatenate([main_q, -main_q], 1).reshape(-1)
    extra = jnp.pad(p[:, 0], (0, a // 2 - pairs))
    extra = jnp.concatenate([extra, extra])
    rest = (padded - pairs - 1) * a
    p_cos = jnp.concatenate([p_rows, extra, jnp.zeros((rest,), F32)])
    p_sin = jnp.concatenate([p_rows, jnp.zeros((a + rest,), F32)])
    q_cos = jnp.pad(q_cos, (0, a + rest))
    return jnp.stack([p_cos, p_sin, q_cos])


def local(
    features,
    coords,
    neighbours,
    live_slots,
    block_count,
    kvec,
    msg_weight,
    filter_weight,
    mlp_in,
    mlp_out,
):
    chans, width = features.shape
    nblocks = width // BLOCK
    regions = lax.axis_size("atoms")
    groups = lax.axis_size("waves")
    here = lax.axis_index("atoms")
    wave = lax.axis_index("waves")
    total = regions * width
    waves_total = kvec.shape[1] * groups
    top = 2 * regions
    a = 2 * top
    pairs = -(-HALF // groups)
    padded = -(-(pairs + 1) // regions) * regions
    first = (wave * pairs).astype(F32)

    h = features
    live = jnp.arange(width, dtype=jnp.int32) < block_count[0] * BLOCK
    masked = jnp.where(live[None, :], h, jnp.zeros_like(h))

    forward = [(i, (i + 1) % regions) for i in range(regions)]
    backward = [((i + 1) % regions, i) for i in range(regions)]
    hm = jnp.dot(msg_weight[0], h, preferred_element_type=F32).astype(BF16)
    hm3 = hm.reshape(chans, nblocks, BLOCK).transpose(1, 0, 2)
    pos3 = coords.reshape(3, nblocks, BLOCK).transpose(1, 0, 2)
    near = jnp.concatenate([lax.ppermute(pos3, "atoms", forward), pos3, lax.ppermute(pos3, "atoms", backward)], 0)
    hm_ext = jnp.concatenate([lax.ppermute(hm3, "atoms", forward), hm3, lax.ppermute(hm3, "atoms", backward)], 0)

    def turns(t, quarter):
        t = t - jnp.round(t)
        return jnp.cos((2.0 * math.pi) * (t - quarter))

    quarter = jnp.array([0.0, 0.25], F32)[:, None, None]
    ka = jnp.arange(1, top + 1, dtype=F32)
    ta = turns((ka[:, None] * coords[0][None, :])[None], quarter).reshape(a, width).astype(BF16)
    b = jnp.arange(top, dtype=F32) + first
    ky = jnp.floor((b + SIDE) / BASE)
    kz = b - ky * BASE
    tb = turns((ky[:, None] * coords[1][None, :] + kz[:, None] * coords[2][None, :])[None], quarter)
    tb = tb.reshape(a, width)

    factor = call(
        functools.partial(structure_kernel, pairs), (padded * a, 2 * chans), F32, [VMEM] * 3, ta, tb, masked
    )
    share = lax.psum_scatter(factor, "atoms", scatter_dimension=0, tiled=True)

    source = neighbours // nblocks
    offset = (source - here) % regions
    which = jnp.where(offset == 0, 1, jnp.where(offset == 1, 2, 0))
    ext_index = which * nblocks + neighbours % nblocks
    mine = nblocks // groups
    slots = neighbours.shape[0]
    extra = -slots % BATCH
    start = wave * mine
    idx = jnp.pad(lax.dynamic_slice_in_dim(ext_index, start, mine, 1), ((0, extra), (0, 0)))
    used = jnp.pad(lax.dynamic_slice_in_dim(live_slots, start, mine, 1), ((0, extra), (0, 0))).astype(F32)
    own = lax.dynamic_slice_in_dim(pos3, start, mine, 0).transpose(0, 2, 1)
    msg = call(
        functools.partial(short_kernel, float(regions)),
        (mine, chans, BLOCK),
        BF16,
        [SMEM, SMEM, VMEM, VMEM, VMEM],
        idx,
        used,
        own,
        near,
        hm_ext,
    )
    msg = lax.all_gather(msg, "waves", axis=0, tiled=True)

    all_k = lax.all_gather(kvec.astype(F32), "waves", axis=1, tiled=True)
    coef = coefficients(all_k, regions, pairs, padded, first)
    owned = padded * a // regions
    coef = lax.dynamic_slice_in_dim(coef, here * owned, owned, 1)
    scaled = share * (1.0 / math.sqrt(total))
    mixing = filter_weight[0]
    cos_part = jnp.dot(scaled[:, :chans], mixing, precision=lax.Precision.HIGHEST)
    sin_part = jnp.dot(scaled[:, chans:], mixing, precision=lax.Precision.HIGHEST)

    def partner(x):
        y = x.reshape(-1, 2, a // 2, chans)
        return jnp.concatenate([y[:, 1:], y[:, :1]], 1).reshape(-1, chans)

    g_cos = coef[0][:, None] * cos_part + coef[2][:, None] * partner(sin_part)
    g_sin = coef[1][:, None] * sin_part - coef[2][:, None] * partner(cos_part)
    filtered = lax.all_gather(jnp.concatenate([g_cos, g_sin], 1).astype(BF16), "atoms", axis=0, tiled=True)

    part = call(
        functools.partial(potentials_kernel, pairs, 1.0 / math.sqrt(waves_total)),
        (chans, width),
        BF16,
        [VMEM] * 3,
        ta,
        tb,
        filtered,
    )
    parts = lax.all_gather(part, "waves", axis=0)
    return call(
        update_kernel,
        (chans, width),
        BF16,
        [SMEM] + [VMEM] * 5,
        block_count,
        h,
        msg,
        parts,
        mlp_in[0],
        mlp_out[0],
    )


def solution(mesh):
    in_specs = (
        P(None, "atoms"),
        P(None, "atoms"),
        P(None, "atoms"),
        P(None, "atoms"),
        P("atoms"),
        P(None, "waves"),
        P(),
        P(),
        P(),
        P(),
    )
    out_specs = P(None, "atoms")
    return jax.shard_map(local, mesh=mesh, in_specs=in_specs, out_specs=out_specs, check_vma=False)
```

```python
import functools
import math

import jax
import jax.numpy as jnp
from jax import lax
from jax.experimental import pallas as pl
from jax.experimental.pallas import tpu as pltpu
from jax.sharding import PartitionSpec as P

BLOCK = 128
MSG_SCALE = 0.125
GAIN_TOP = 20.0
SIDE = 5
BASE = 2 * SIDE + 1
HALF = (BASE * BASE + 1) // 2
BATCH = 4
F32 = jnp.float32
BF16 = jnp.bfloat16
VMEM = pl.BlockSpec(memory_space=pltpu.VMEM)
SMEM = pl.BlockSpec(memory_space=pltpu.SMEM)
NT = (((1,), (1,)), ((), ()))
TN = (((0,), (0,)), ((), ()))
DMA = pltpu.SemaphoreType.DMA


def phase_rows(ta, tb_ref, pair, held):
    half = tb_ref.shape[0] // 2
    cb = tb_ref[pl.ds(pair, 1), :].astype(BF16)
    sb = tb_ref[pl.ds(half + pair, 1), :].astype(BF16)
    return ta * cb, ta * sb


def groups_of(count):
    return [(i, min(4, count - i)) for i in range(0, count, 4)]


MESH = pl.DeviceIdType.MESH


def meet(peers):
    barrier = pltpu.get_barrier_semaphore()
    for peer in peers:
        pl.semaphore_signal(barrier, inc=1, device_id=peer, device_id_type=MESH)
    pl.semaphore_wait(barrier, len(peers))


def others(axis):
    count = lax.axis_size(axis)
    me = lax.axis_index(axis)
    return [{axis: lax.rem(me + d, count)} for d in range(1, count)]


def send(src, dst, sends, receives, slot, peer):
    copy = pltpu.make_async_remote_copy(
        src_ref=src,
        dst_ref=dst,
        send_sem=sends.at[slot],
        recv_sem=receives.at[slot],
        device_id=peer,
        device_id_type=MESH,
    )
    copy.start()
    return copy


def structure_kernel(
    pairs, ta_ref, tb_ref, h_ref, pos_ref, hm_ref, k_ref, out_ref, near_ref, ext_ref, allk_ref, sends, receives
):
    a = ta_ref.shape[0]
    nblocks = pos_ref.shape[0]
    regions = lax.axis_size("atoms")
    here = lax.axis_index("atoms")
    wave = lax.axis_index("waves")
    right = {"atoms": lax.rem(here + 1, regions)}
    left = {"atoms": lax.rem(here + regions - 1, regions)}
    waves = others("waves")
    meet([left, right] + waves)
    copies = []
    for side, peer in ((0, right), (2, left)):
        place = pl.ds(side * nblocks, nblocks)
        copies.append(send(hm_ref, ext_ref.at[place], sends, receives, len(copies), peer))
        copies.append(send(pos_ref, near_ref.at[place], sends, receives, len(copies), peer))
    for peer in waves:
        copies.append(send(k_ref, allk_ref.at[wave], sends, receives, len(copies), peer))
    ext_ref[nblocks : 2 * nblocks] = hm_ref[...]
    near_ref[nblocks : 2 * nblocks] = pos_ref[...]
    allk_ref[wave] = k_ref[...]

    ta = ta_ref[...]
    h = h_ref[...]
    for first, size in groups_of(pairs):
        cs, ss = zip(*[phase_rows(ta, tb_ref, first + i, pairs) for i in range(size)])
        rows = slice(first * a, (first + size) * a)
        c = lax.dot_general(jnp.concatenate(cs, 0), h, NT, preferred_element_type=F32)
        s = lax.dot_general(jnp.concatenate(ss, 0), h, NT, preferred_element_type=F32)
        out_ref[rows, :] = jnp.concatenate([c, s], 1).astype(BF16)
    c = lax.dot_general(tb_ref[...].astype(BF16), h, NT, preferred_element_type=F32)
    out_ref[pairs * a : (pairs + 1) * a, :] = jnp.concatenate([c, jnp.zeros_like(c)], 1).astype(BF16)
    rest = out_ref.shape[0] - (pairs + 1) * a
    if rest:
        out_ref[(pairs + 1) * a :, :] = jnp.zeros((rest, out_ref.shape[1]), BF16)
    for copy in copies:
        copy.wait()


def exchange_kernel(
    scale_x,
    scale,
    a,
    idx_ref,
    live_ref,
    factor_ref,
    p_ref,
    q_ref,
    same_ref,
    cross_ref,
    own_ref,
    near_ref,
    hm_ref,
    out_ref,
    msg_ref,
    inbox,
    sends,
    receives,
    sends2,
    receives2,
):
    here = lax.axis_index("atoms")
    peers = others("atoms")
    meet(peers)
    copies = [
        send(factor_ref.at[peer["atoms"]], inbox.at[d], sends, receives, d, peer) for d, peer in enumerate(peers)
    ]
    blocks = own_ref.shape[0]
    early = blocks // 2
    short_blocks(scale_x, 0, early, idx_ref, live_ref, own_ref, near_ref, hm_ref, msg_ref)
    for copy in copies:
        copy.wait()
    total = factor_ref[here].astype(F32)
    for d in range(len(peers)):
        total = total + inbox[d].astype(F32)
    total = total * scale
    half = a // 2
    parts = []
    for row in range(0, total.shape[0], a):
        parts += [total[row + half : row + a], total[row : row + half]]
    partner = jnp.concatenate(parts, 0)
    high = lax.Precision.HIGHEST
    mixed = jnp.dot(total, same_ref[...], precision=high, preferred_element_type=F32)
    crossed = jnp.dot(partner, cross_ref[...], precision=high, preferred_element_type=F32)
    out_ref[here] = (p_ref[...] * mixed + q_ref[...] * crossed).astype(BF16)
    copies = [
        send(out_ref.at[here], out_ref.at[here], sends2, receives2, d, peer) for d, peer in enumerate(peers)
    ]
    short_blocks(scale_x, early, blocks, idx_ref, live_ref, own_ref, near_ref, hm_ref, msg_ref)
    for copy in copies:
        copy.wait()


def finish_kernel(
    pairs,
    scale,
    count_ref,
    ta_ref,
    tb_ref,
    g_ref,
    h_ref,
    mine_ref,
    first_ref,
    second_ref,
    out_ref,
    msg_ref,
    pot_ref,
    sends,
    receives,
):
    wave = lax.axis_index("waves")
    peers = others("waves")
    count = len(peers)
    meet(peers)
    msg_ref[wave] = mine_ref[...]
    copies = [
        send(mine_ref, msg_ref.at[wave], sends, receives, d, peer) for d, peer in enumerate(peers)
    ]
    a = ta_ref.shape[0]
    ta = ta_ref[...]
    rows = tb_ref.shape[0]
    acc = lax.dot_general(
        g_ref[pairs * a : pairs * a + rows, 0:64], tb_ref[...].astype(BF16), TN, preferred_element_type=F32
    )
    for first, size in groups_of(pairs):
        cs, ss = zip(*[phase_rows(ta, tb_ref, first + i, pairs) for i in range(size)])
        g = g_ref[first * a : (first + size) * a, :]
        acc += lax.dot_general(g[:, 0:64], jnp.concatenate(cs, 0), TN, preferred_element_type=F32)
        acc += lax.dot_general(g[:, 64:128], jnp.concatenate(ss, 0), TN, preferred_element_type=F32)
    pot_ref[wave] = (acc * scale).astype(BF16)
    copies += [
        send(pot_ref.at[wave], pot_ref.at[wave], sends, receives, count + d, peer) for d, peer in enumerate(peers)
    ]
    for copy in copies:
        copy.wait()
    h = h_ref[...]
    pot = pot_ref[0].astype(F32)
    for w in range(1, pot_ref.shape[0]):
        pot = pot + pot_ref[w].astype(F32)
    msg = jnp.concatenate(
        [msg_ref[w, b] for w in range(msg_ref.shape[0]) for b in range(msg_ref.shape[1])], 1
    )
    z = jnp.concatenate([h, msg, pot.astype(BF16)], 0)
    hidden = jnp.dot(first_ref[...], z, preferred_element_type=F32)
    hidden = (hidden * jax.nn.sigmoid(hidden)).astype(BF16)
    out = h.astype(F32) + jnp.dot(second_ref[...], hidden, preferred_element_type=F32)
    atom = lax.broadcasted_iota(jnp.int32, out.shape, 1)
    out_ref[...] = jnp.where(atom < count_ref[0] * BLOCK, out, 0.0).astype(BF16)


def short_blocks(scale_x, begin, end, idx_ref, live_ref, own_ref, near_ref, hm_ref, out_ref):
    steps = idx_ref.shape[0] // BATCH

    def block_step(b, _):
        own = own_ref[b]
        cols = [jnp.broadcast_to(own[:, d : d + 1], (BLOCK, BLOCK)) for d in range(3)]

        def slot_step(step, acc):
            weights, mapped = [], []
            for u in range(BATCH):
                s = step * BATCH + u
                n = idx_ref[s, b]
                near = near_ref[n]
                total = None
                for d in (1, 2, 0):
                    diff = cols[d] - near[d : d + 1, :]
                    diff = diff - jnp.round(diff)
                    if d == 0:
                        diff = diff * scale_x
                    total = diff * diff if total is None else total + diff * diff
                weights.append(jnp.exp2(total * (-2.0 * math.log2(math.e))).astype(BF16))
                mapped.append(hm_ref[n] * live_ref[s, b].astype(BF16))
            return acc + lax.dot_general(
                jnp.concatenate(mapped, 1), jnp.concatenate(weights, 1), NT, preferred_element_type=F32
            )

        acc = lax.fori_loop(0, steps, slot_step, jnp.zeros((hm_ref.shape[1], BLOCK), F32))
        out_ref[b] = (acc * MSG_SCALE).astype(BF16)
        return 0

    lax.fori_loop(begin, end, block_step, 0)


def call(kernel, ident, shapes, specs, scratch, *args):
    return pl.pallas_call(
        kernel,
        out_shape=[jax.ShapeDtypeStruct(shape, dtype) for shape, dtype in shapes],
        in_specs=specs,
        out_specs=[VMEM] * len(shapes),
        scratch_shapes=scratch,
        compiler_params=pltpu.CompilerParams(
            vmem_limit_bytes=48 * 1024 * 1024, collective_id=ident, has_side_effects=True
        ),
    )(*args)


def coefficients(kvec, regions, pairs, padded, first, here, owned, chans):
    top = 2 * regions
    k = jnp.where(kvec[0:1] < 0, -kvec, kvec)
    code = k[1] * BASE + k[2]
    n = jnp.abs(code) - first
    onehot_a = (jnp.arange(top + 1, dtype=F32)[:, None] == k[0][None, :]).astype(BF16)
    which = jnp.arange(pairs, dtype=F32)[:, None] == n[None, :]
    up = (which & (code >= 0)[None, :]).astype(BF16)
    down = (which & (code < 0)[None, :]).astype(BF16)
    m1 = lax.dot_general(up, onehot_a, NT, preferred_element_type=F32)
    m2 = lax.dot_general(down, onehot_a, NT, preferred_element_type=F32)
    b = jnp.arange(pairs, dtype=F32) + first
    ky = jnp.floor((b + SIDE) / BASE)
    kz = b - ky * BASE
    kx = jnp.arange(top + 1, dtype=F32) / regions
    gain = GAIN_TOP / (4.0 + (kx * kx)[None, :] + (ky * ky + kz * kz)[:, None])
    p = gain * (m1 + m2)
    q = gain * (m2 - m1)
    main_p, main_q = p[:, 1:], q[:, 1:]
    a = 2 * top
    p_rows = jnp.concatenate([main_p, main_p], 1).reshape(-1)
    q_cos = jnp.concatenate([main_q, -main_q], 1).reshape(-1)
    extra = jnp.pad(p[:, 0], (0, a // 2 - pairs))
    extra = jnp.concatenate([extra, extra])
    rest = (padded - pairs - 1) * a
    p_cos = jnp.concatenate([p_rows, extra, jnp.zeros((rest,), F32)])
    p_sin = jnp.concatenate([p_rows, jnp.zeros((a + rest,), F32)])
    q_cos = jnp.pad(q_cos, (0, a + rest))
    p_cos, p_sin, q_cos = [lax.dynamic_slice_in_dim(x, here * owned, owned, 0) for x in (p_cos, p_sin, q_cos)]
    wide = lambda x, y: jnp.concatenate(
        [jnp.broadcast_to(v[:, None], (owned, chans)) for v in (x, y)], 1
    )
    return wide(p_cos, p_sin), wide(q_cos, -q_cos)


def local(
    features,
    coords,
    neighbours,
    live_slots,
    block_count,
    kvec,
    msg_weight,
    filter_weight,
    mlp_in,
    mlp_out,
):
    chans, width = features.shape
    nblocks = width // BLOCK
    regions = lax.axis_size("atoms")
    groups = lax.axis_size("waves")
    here = lax.axis_index("atoms")
    wave = lax.axis_index("waves")
    total = regions * width
    waves_total = kvec.shape[1] * groups
    top = 2 * regions
    a = 2 * top
    pairs = -(-HALF // groups)
    padded = -(-(pairs + 1) // regions) * regions
    first = (wave * pairs).astype(F32)

    h = features
    live = jnp.arange(width, dtype=jnp.int32) < block_count[0] * BLOCK
    masked = jnp.where(live[None, :], h, jnp.zeros_like(h))

    hm = jnp.dot(msg_weight[0], h, preferred_element_type=F32).astype(BF16)
    hm3 = hm.reshape(chans, nblocks, BLOCK).transpose(1, 0, 2)
    pos3 = coords.reshape(3, nblocks, BLOCK).transpose(1, 0, 2)

    def turns(t, quarter):
        t = t - jnp.round(t)
        return jnp.cos((2.0 * math.pi) * (t - quarter))

    quarter = jnp.array([0.0, 0.25], F32)[:, None, None]
    ka = jnp.arange(1, top + 1, dtype=F32)
    ta = turns((ka[:, None] * coords[0][None, :])[None], quarter).reshape(a, width).astype(BF16)
    b = jnp.arange(top, dtype=F32) + first
    ky = jnp.floor((b + SIDE) / BASE)
    kz = b - ky * BASE
    tb = turns((ky[:, None] * coords[1][None, :] + kz[:, None] * coords[2][None, :])[None], quarter)
    tb = tb.reshape(a, width)

    copies = 4 + groups - 1
    factor, near, hm_ext, all_k = call(
        functools.partial(structure_kernel, pairs),
        0,
        [
            ((padded * a, 2 * chans), BF16),
            ((3 * nblocks, 3, BLOCK), F32),
            ((3 * nblocks, chans, BLOCK), BF16),
            ((groups,) + kvec.shape, F32),
        ],
        [VMEM] * 6,
        [DMA((copies,)), DMA((copies,))],
        ta,
        tb,
        masked,
        pos3,
        hm3,
        kvec.astype(F32),
    )
    all_k = all_k.transpose(1, 0, 2).reshape(kvec.shape[0], -1)

    source = neighbours // nblocks
    offset = (source - here) % regions
    which = jnp.where(offset == 0, 1, jnp.where(offset == 1, 2, 0))
    ext_index = which * nblocks + neighbours % nblocks
    mine = nblocks // groups
    slots = neighbours.shape[0]
    extra = -slots % BATCH
    start = wave * mine
    idx = jnp.pad(lax.dynamic_slice_in_dim(ext_index, start, mine, 1), ((0, extra), (0, 0)))
    used = jnp.pad(lax.dynamic_slice_in_dim(live_slots, start, mine, 1), ((0, extra), (0, 0))).astype(F32)
    own = lax.dynamic_slice_in_dim(pos3, start, mine, 0).transpose(0, 2, 1)
    owned = padded * a // regions
    p, q = coefficients(all_k, regions, pairs, padded, first, here, owned, chans)
    mixing = filter_weight[0]
    zero = jnp.zeros_like(mixing)
    same = jnp.block([[mixing, zero], [zero, mixing]])
    cross = jnp.block([[zero, mixing], [mixing, zero]])
    peers = regions - 1
    filtered, msg = call(
        functools.partial(exchange_kernel, float(regions), 1.0 / math.sqrt(total), a),
        1,
        [((regions, owned, 2 * chans), BF16), ((mine, chans, BLOCK), BF16)],
        [SMEM] * 2 + [VMEM] * 8,
        [pltpu.VMEM((peers, owned, 2 * chans), BF16)] + [DMA((peers,))] * 4,
        idx,
        used,
        factor.reshape(regions, owned, 2 * chans),
        p,
        q,
        same,
        cross,
        own,
        near,
        hm_ext,
    )
    peers = groups - 1
    return call(
        functools.partial(finish_kernel, pairs, 1.0 / math.sqrt(waves_total)),
        2,
        [((chans, width), BF16)],
        [SMEM] + [VMEM] * 7,
        [pltpu.VMEM((groups, mine, chans, BLOCK), BF16), pltpu.VMEM((groups, chans, width), BF16)]
        + [DMA((2 * peers,))] * 2,
        block_count,
        ta,
        tb,
        filtered.reshape(padded * a, 2 * chans),
        h,
        msg,
        mlp_in[0],
        mlp_out[0],
    )[0]


def solution(mesh):
    in_specs = (
        P(None, "atoms"),
        P(None, "atoms"),
        P(None, "atoms"),
        P(None, "atoms"),
        P("atoms"),
        P(None, "waves"),
        P(),
        P(),
        P(),
        P(),
    )
    out_specs = P(None, "atoms")
    return jax.shard_map(local, mesh=mesh, in_specs=in_specs, out_specs=out_specs, check_vma=False)
```

```python
import functools
import math

import jax
import jax.numpy as jnp
from jax import lax
from jax.experimental import pallas as pl
from jax.experimental.pallas import tpu as pltpu
from jax.sharding import PartitionSpec as P

BLOCK = 128
MSG_SCALE = 0.125
GAIN_TOP = 20.0
SIDE = 5
BASE = 2 * SIDE + 1
HALF = (BASE * BASE + 1) // 2
BATCH = 7
F32 = jnp.float32
BF16 = jnp.bfloat16
VMEM = pl.BlockSpec(memory_space=pltpu.VMEM)
SMEM = pl.BlockSpec(memory_space=pltpu.SMEM)
NT = (((1,), (1,)), ((), ()))
TN = (((0,), (0,)), ((), ()))
DMA = pltpu.SemaphoreType.DMA


def phase_rows(ta, tb_ref, pair, held):
    half = tb_ref.shape[0] // 2
    cb = tb_ref[pl.ds(pair, 1), :].astype(BF16)
    sb = tb_ref[pl.ds(half + pair, 1), :].astype(BF16)
    return ta * cb, ta * sb


def groups_of(count):
    return [(i, min(4, count - i)) for i in range(0, count, 4)]


MESH = pl.DeviceIdType.MESH


def meet(peers):
    barrier = pltpu.get_barrier_semaphore()
    for peer in peers:
        pl.semaphore_signal(barrier, inc=1, device_id=peer, device_id_type=MESH)
    pl.semaphore_wait(barrier, len(peers))


def others(axis):
    count = lax.axis_size(axis)
    me = lax.axis_index(axis)
    return [{axis: lax.rem(me + d, count)} for d in range(1, count)]


def send(src, dst, sends, receives, slot, peer):
    copy = pltpu.make_async_remote_copy(
        src_ref=src,
        dst_ref=dst,
        send_sem=sends.at[slot],
        recv_sem=receives.at[slot],
        device_id=peer,
        device_id_type=MESH,
    )
    copy.start()
    return copy


def structure_kernel(
    pairs, ta_ref, tb_ref, h_ref, pos_ref, hm_ref, k_ref, out_ref, near_ref, ext_ref, allk_ref, sends, receives
):
    a = ta_ref.shape[0]
    nblocks = pos_ref.shape[0]
    regions = lax.axis_size("atoms")
    here = lax.axis_index("atoms")
    wave = lax.axis_index("waves")
    right = {"atoms": lax.rem(here + 1, regions)}
    left = {"atoms": lax.rem(here + regions - 1, regions)}
    waves = others("waves")
    meet([left, right] + waves)
    copies = []
    for side, peer in ((0, right), (2, left)):
        place = pl.ds(side * nblocks, nblocks)
        copies.append(send(hm_ref, ext_ref.at[place], sends, receives, len(copies), peer))
        copies.append(send(pos_ref, near_ref.at[place], sends, receives, len(copies), peer))
    for peer in waves:
        copies.append(send(k_ref, allk_ref.at[wave], sends, receives, len(copies), peer))
    ext_ref[nblocks : 2 * nblocks] = hm_ref[...]
    near_ref[nblocks : 2 * nblocks] = pos_ref[...]
    allk_ref[wave] = k_ref[...]

    ta = ta_ref[...]
    h = h_ref[...]
    for first, size in groups_of(pairs):
        cs, ss = zip(*[phase_rows(ta, tb_ref, first + i, pairs) for i in range(size)])
        rows = slice(first * a, (first + size) * a)
        c = lax.dot_general(jnp.concatenate(cs, 0), h, NT, preferred_element_type=F32)
        s = lax.dot_general(jnp.concatenate(ss, 0), h, NT, preferred_element_type=F32)
        out_ref[rows, :] = jnp.concatenate([c, s], 1).astype(BF16)
    c = lax.dot_general(tb_ref[...].astype(BF16), h, NT, preferred_element_type=F32)
    out_ref[pairs * a : (pairs + 1) * a, :] = jnp.concatenate([c, jnp.zeros_like(c)], 1).astype(BF16)
    rest = out_ref.shape[0] - (pairs + 1) * a
    if rest:
        out_ref[(pairs + 1) * a :, :] = jnp.zeros((rest, out_ref.shape[1]), BF16)
    for copy in copies:
        copy.wait()


def exchange_kernel(
    scale_x,
    scale,
    a,
    idx_ref,
    live_ref,
    factor_ref,
    p_ref,
    q_ref,
    same_ref,
    cross_ref,
    own_ref,
    near_ref,
    hm_ref,
    out_ref,
    msg_ref,
    inbox,
    sends,
    receives,
    sends2,
    receives2,
):
    here = lax.axis_index("atoms")
    peers = others("atoms")
    meet(peers)
    copies = [
        send(factor_ref.at[peer["atoms"]], inbox.at[d], sends, receives, d, peer) for d, peer in enumerate(peers)
    ]
    blocks = own_ref.shape[0]
    early = blocks // 2
    short_blocks(scale_x, 0, early, idx_ref, live_ref, own_ref, near_ref, hm_ref, msg_ref)
    for copy in copies:
        copy.wait()
    total = factor_ref[here].astype(F32)
    for d in range(len(peers)):
        total = total + inbox[d].astype(F32)
    total = total * scale
    half = a // 2
    parts = []
    for row in range(0, total.shape[0], a):
        parts += [total[row + half : row + a], total[row : row + half]]
    partner = jnp.concatenate(parts, 0)
    high = lax.Precision.HIGHEST
    mixed = jnp.dot(total, same_ref[...], precision=high, preferred_element_type=F32)
    crossed = jnp.dot(partner, cross_ref[...], precision=high, preferred_element_type=F32)
    out_ref[here] = (p_ref[...] * mixed + q_ref[...] * crossed).astype(BF16)
    copies = [
        send(out_ref.at[here], out_ref.at[here], sends2, receives2, d, peer) for d, peer in enumerate(peers)
    ]
    short_blocks(scale_x, early, blocks, idx_ref, live_ref, own_ref, near_ref, hm_ref, msg_ref)
    for copy in copies:
        copy.wait()


def finish_kernel(
    pairs,
    scale,
    count_ref,
    ta_ref,
    tb_ref,
    g_ref,
    h_ref,
    mine_ref,
    first_ref,
    second_ref,
    out_ref,
    msg_ref,
    pot_ref,
    sends,
    receives,
):
    wave = lax.axis_index("waves")
    peers = others("waves")
    count = len(peers)
    meet(peers)
    msg_ref[wave] = mine_ref[...]
    copies = [
        send(mine_ref, msg_ref.at[wave], sends, receives, d, peer) for d, peer in enumerate(peers)
    ]
    a = ta_ref.shape[0]
    ta = ta_ref[...]
    rows = tb_ref.shape[0]
    acc = lax.dot_general(
        g_ref[pairs * a : pairs * a + rows, 0:64], tb_ref[...].astype(BF16), TN, preferred_element_type=F32
    )
    for first, size in groups_of(pairs):
        cs, ss = zip(*[phase_rows(ta, tb_ref, first + i, pairs) for i in range(size)])
        g = g_ref[first * a : (first + size) * a, :]
        acc += lax.dot_general(g[:, 0:64], jnp.concatenate(cs, 0), TN, preferred_element_type=F32)
        acc += lax.dot_general(g[:, 64:128], jnp.concatenate(ss, 0), TN, preferred_element_type=F32)
    pot_ref[wave] = (acc * scale).astype(BF16)
    copies += [
        send(pot_ref.at[wave], pot_ref.at[wave], sends, receives, count + d, peer) for d, peer in enumerate(peers)
    ]
    for copy in copies:
        copy.wait()
    h = h_ref[...]
    pot = pot_ref[0].astype(F32)
    for w in range(1, pot_ref.shape[0]):
        pot = pot + pot_ref[w].astype(F32)
    msg = jnp.concatenate(
        [msg_ref[w, b] for w in range(msg_ref.shape[0]) for b in range(msg_ref.shape[1])], 1
    )
    z = jnp.concatenate([h, msg, pot.astype(BF16)], 0)
    hidden = jnp.dot(first_ref[...], z, preferred_element_type=F32)
    hidden = (hidden * jax.nn.sigmoid(hidden)).astype(BF16)
    out = h.astype(F32) + jnp.dot(second_ref[...], hidden, preferred_element_type=F32)
    atom = lax.broadcasted_iota(jnp.int32, out.shape, 1)
    out_ref[...] = jnp.where(atom < count_ref[0] * BLOCK, out, 0.0).astype(BF16)


def short_blocks(scale_x, begin, end, idx_ref, live_ref, own_ref, near_ref, hm_ref, out_ref):
    steps = idx_ref.shape[0] // BATCH

    def block_step(b, _):
        own = own_ref[b]
        cols = [jnp.broadcast_to(own[:, d : d + 1], (BLOCK, BLOCK)) for d in range(3)]

        def slot_step(step, acc):
            weights, mapped = [], []
            for u in range(BATCH):
                s = step * BATCH + u
                n = idx_ref[s, b]
                near = near_ref[n]
                total = None
                for d in (1, 2, 0):
                    diff = cols[d] - near[d : d + 1, :]
                    diff = diff - jnp.round(diff)
                    if d == 0:
                        diff = diff * scale_x
                    total = diff * diff if total is None else total + diff * diff
                weights.append(jnp.exp2(total * (-2.0 * math.log2(math.e))).astype(BF16))
                mapped.append(hm_ref[n] * live_ref[s, b].astype(BF16))
            return acc + lax.dot_general(
                jnp.concatenate(weights, 1), jnp.concatenate(mapped, 1), NT, preferred_element_type=F32
            )

        acc = lax.fori_loop(0, steps, slot_step, jnp.zeros((BLOCK, hm_ref.shape[1]), F32))
        out_ref[b] = (acc * MSG_SCALE).T.astype(BF16)
        return 0

    lax.fori_loop(begin, end, block_step, 0)


def call(kernel, ident, shapes, specs, scratch, *args):
    return pl.pallas_call(
        kernel,
        out_shape=[jax.ShapeDtypeStruct(shape, dtype) for shape, dtype in shapes],
        in_specs=specs,
        out_specs=[VMEM] * len(shapes),
        scratch_shapes=scratch,
        compiler_params=pltpu.CompilerParams(
            vmem_limit_bytes=48 * 1024 * 1024, collective_id=ident, has_side_effects=True
        ),
    )(*args)


def coefficients(kvec, regions, pairs, padded, first, here, owned, chans):
    top = 2 * regions
    k = jnp.where(kvec[0:1] < 0, -kvec, kvec)
    code = k[1] * BASE + k[2]
    n = jnp.abs(code) - first
    onehot_a = (jnp.arange(top + 1, dtype=F32)[:, None] == k[0][None, :]).astype(BF16)
    which = jnp.arange(pairs, dtype=F32)[:, None] == n[None, :]
    up = (which & (code >= 0)[None, :]).astype(BF16)
    down = (which & (code < 0)[None, :]).astype(BF16)
    m1 = lax.dot_general(up, onehot_a, NT, preferred_element_type=F32)
    m2 = lax.dot_general(down, onehot_a, NT, preferred_element_type=F32)
    b = jnp.arange(pairs, dtype=F32) + first
    ky = jnp.floor((b + SIDE) / BASE)
    kz = b - ky * BASE
    kx = jnp.arange(top + 1, dtype=F32) / regions
    gain = GAIN_TOP / (4.0 + (kx * kx)[None, :] + (ky * ky + kz * kz)[:, None])
    p = gain * (m1 + m2)
    q = gain * (m2 - m1)
    main_p, main_q = p[:, 1:], q[:, 1:]
    a = 2 * top
    p_rows = jnp.concatenate([main_p, main_p], 1).reshape(-1)
    q_cos = jnp.concatenate([main_q, -main_q], 1).reshape(-1)
    extra = jnp.pad(p[:, 0], (0, a // 2 - pairs))
    extra = jnp.concatenate([extra, extra])
    rest = (padded - pairs - 1) * a
    p_cos = jnp.concatenate([p_rows, extra, jnp.zeros((rest,), F32)])
    p_sin = jnp.concatenate([p_rows, jnp.zeros((a + rest,), F32)])
    q_cos = jnp.pad(q_cos, (0, a + rest))
    p_cos, p_sin, q_cos = [lax.dynamic_slice_in_dim(x, here * owned, owned, 0) for x in (p_cos, p_sin, q_cos)]
    wide = lambda x, y: jnp.concatenate(
        [jnp.broadcast_to(v[:, None], (owned, chans)) for v in (x, y)], 1
    )
    return wide(p_cos, p_sin), wide(q_cos, -q_cos)


def local(
    features,
    coords,
    neighbours,
    live_slots,
    block_count,
    kvec,
    msg_weight,
    filter_weight,
    mlp_in,
    mlp_out,
):
    chans, width = features.shape
    nblocks = width // BLOCK
    regions = lax.axis_size("atoms")
    groups = lax.axis_size("waves")
    here = lax.axis_index("atoms")
    wave = lax.axis_index("waves")
    total = regions * width
    waves_total = kvec.shape[1] * groups
    top = 2 * regions
    a = 2 * top
    pairs = -(-HALF // groups)
    padded = -(-(pairs + 1) // regions) * regions
    first = (wave * pairs).astype(F32)

    h = features
    live = jnp.arange(width, dtype=jnp.int32) < block_count[0] * BLOCK
    masked = jnp.where(live[None, :], h, jnp.zeros_like(h))

    hm = jnp.dot(msg_weight[0], h, preferred_element_type=F32).astype(BF16)
    hm3 = hm.reshape(chans, nblocks, BLOCK).transpose(1, 0, 2)
    pos3 = coords.reshape(3, nblocks, BLOCK).transpose(1, 0, 2)

    def turns(t, quarter):
        t = t - jnp.round(t)
        return jnp.cos((2.0 * math.pi) * (t - quarter))

    quarter = jnp.array([0.0, 0.25], F32)[:, None, None]
    ka = jnp.arange(1, top + 1, dtype=F32)
    ta = turns((ka[:, None] * coords[0][None, :])[None], quarter).reshape(a, width).astype(BF16)
    b = jnp.arange(top, dtype=F32) + first
    ky = jnp.floor((b + SIDE) / BASE)
    kz = b - ky * BASE
    tb = turns((ky[:, None] * coords[1][None, :] + kz[:, None] * coords[2][None, :])[None], quarter)
    tb = tb.reshape(a, width)

    copies = 4 + groups - 1
    factor, near, hm_ext, all_k = call(
        functools.partial(structure_kernel, pairs),
        0,
        [
            ((padded * a, 2 * chans), BF16),
            ((3 * nblocks, 3, BLOCK), F32),
            ((3 * nblocks, chans, BLOCK), BF16),
            ((groups,) + kvec.shape, F32),
        ],
        [VMEM] * 6,
        [DMA((copies,)), DMA((copies,))],
        ta,
        tb,
        masked,
        pos3,
        hm3,
        kvec.astype(F32),
    )
    all_k = all_k.transpose(1, 0, 2).reshape(kvec.shape[0], -1)

    source = neighbours // nblocks
    offset = (source - here) % regions
    which = jnp.where(offset == 0, 1, jnp.where(offset == 1, 2, 0))
    ext_index = which * nblocks + neighbours % nblocks
    mine = nblocks // groups
    slots = neighbours.shape[0]
    extra = -slots % BATCH
    start = wave * mine
    idx = jnp.pad(lax.dynamic_slice_in_dim(ext_index, start, mine, 1), ((0, extra), (0, 0)))
    used = jnp.pad(lax.dynamic_slice_in_dim(live_slots, start, mine, 1), ((0, extra), (0, 0))).astype(F32)
    own = lax.dynamic_slice_in_dim(pos3, start, mine, 0).transpose(0, 2, 1)
    owned = padded * a // regions
    p, q = coefficients(all_k, regions, pairs, padded, first, here, owned, chans)
    mixing = filter_weight[0]
    zero = jnp.zeros_like(mixing)
    same = jnp.block([[mixing, zero], [zero, mixing]])
    cross = jnp.block([[zero, mixing], [mixing, zero]])
    peers = regions - 1
    filtered, msg = call(
        functools.partial(exchange_kernel, float(regions), 1.0 / math.sqrt(total), a),
        1,
        [((regions, owned, 2 * chans), BF16), ((mine, chans, BLOCK), BF16)],
        [SMEM] * 2 + [VMEM] * 8,
        [pltpu.VMEM((peers, owned, 2 * chans), BF16)] + [DMA((peers,))] * 4,
        idx,
        used,
        factor.reshape(regions, owned, 2 * chans),
        p,
        q,
        same,
        cross,
        own,
        near,
        hm_ext,
    )
    peers = groups - 1
    return call(
        functools.partial(finish_kernel, pairs, 1.0 / math.sqrt(waves_total)),
        2,
        [((chans, width), BF16)],
        [SMEM] + [VMEM] * 7,
        [pltpu.VMEM((groups, mine, chans, BLOCK), BF16), pltpu.VMEM((groups, chans, width), BF16)]
        + [DMA((2 * peers,))] * 2,
        block_count,
        ta,
        tb,
        filtered.reshape(padded * a, 2 * chans),
        h,
        msg,
        mlp_in[0],
        mlp_out[0],
    )[0]


def solution(mesh):
    in_specs = (
        P(None, "atoms"),
        P(None, "atoms"),
        P(None, "atoms"),
        P(None, "atoms"),
        P("atoms"),
        P(None, "waves"),
        P(),
        P(),
        P(),
        P(),
    )
    out_specs = P(None, "atoms")
    return jax.shard_map(local, mesh=mesh, in_specs=in_specs, out_specs=out_specs, check_vma=False)
```

```python
import functools
import math

import jax
import jax.numpy as jnp
from jax import lax
from jax.experimental import pallas as pl
from jax.experimental.pallas import tpu as pltpu
from jax.sharding import PartitionSpec as P

BLOCK = 128
MSG_SCALE = 0.125
GAIN_TOP = 20.0
SIDE = 5
BASE = 2 * SIDE + 1
HALF = (BASE * BASE + 1) // 2
BATCH = 4
CHUNK = 256
COS = [(-1.0) ** n * (2.0 * math.pi) ** (2 * n) / math.factorial(2 * n) for n in range(10)]
F32 = jnp.float32
BF16 = jnp.bfloat16
VMEM = pl.BlockSpec(memory_space=pltpu.VMEM)
SMEM = pl.BlockSpec(memory_space=pltpu.SMEM)
NT = (((1,), (1,)), ((), ()))
TN = (((0,), (0,)), ((), ()))
DMA = pltpu.SemaphoreType.DMA


def phase_rows(ta, tb_ref, pair, held):
    half = tb_ref.shape[0] // 2
    cb = tb_ref[pl.ds(pair, 1), :].astype(BF16)
    sb = tb_ref[pl.ds(half + pair, 1), :].astype(BF16)
    return ta * cb, ta * sb


def groups_of(count):
    return [(i, min(4, count - i)) for i in range(0, count, 4)]


MESH = pl.DeviceIdType.MESH


def meet(peers):
    barrier = pltpu.get_barrier_semaphore()
    for peer in peers:
        pl.semaphore_signal(barrier, inc=1, device_id=peer, device_id_type=MESH)
    pl.semaphore_wait(barrier, len(peers))


def others(axis):
    count = lax.axis_size(axis)
    me = lax.axis_index(axis)
    return [{axis: lax.rem(me + d, count)} for d in range(1, count)]


def send(src, dst, sends, receives, slot, peer):
    copy = pltpu.make_async_remote_copy(
        src_ref=src,
        dst_ref=dst,
        send_sem=sends.at[slot],
        recv_sem=receives.at[slot],
        device_id=peer,
        device_id_type=MESH,
    )
    copy.start()
    return copy


def cos_turns(u):
    w = u * u
    out = COS[-1] * w + COS[-2]
    for c in COS[-3::-1]:
        out = out * w + c
    return out


def cos_sin(t):
    t = t - jnp.round(t)
    shifted = t - 0.25
    return cos_turns(t), cos_turns(shifted - jnp.round(shifted))


def structure_kernel(
    pairs,
    coords_ref,
    h_ref,
    pos_ref,
    hm_ref,
    k_ref,
    out_ref,
    near_ref,
    ext_ref,
    allk_ref,
    ta_ref,
    tb_ref,
    sends,
    receives,
):
    a = ta_ref.shape[0]
    top = a // 2
    nblocks = pos_ref.shape[0]
    regions = lax.axis_size("atoms")
    here = lax.axis_index("atoms")
    wave = lax.axis_index("waves")
    right = {"atoms": lax.rem(here + 1, regions)}
    left = {"atoms": lax.rem(here + regions - 1, regions)}
    waves = others("waves")
    meet([left, right] + waves)
    copies = []
    for side, peer in ((0, right), (2, left)):
        place = pl.ds(side * nblocks, nblocks)
        copies.append(send(hm_ref, ext_ref.at[place], sends, receives, len(copies), peer))
        copies.append(send(pos_ref, near_ref.at[place], sends, receives, len(copies), peer))
    for peer in waves:
        copies.append(send(k_ref, allk_ref.at[wave], sends, receives, len(copies), peer))
    ext_ref[nblocks : 2 * nblocks] = hm_ref[...]
    near_ref[nblocks : 2 * nblocks] = pos_ref[...]
    allk_ref[wave] = k_ref[...]

    ka = lax.broadcasted_iota(jnp.int32, (top, CHUNK), 0).astype(F32)
    b = ka + (wave * pairs).astype(F32)
    ka = ka + 1.0
    ky = jnp.floor((b + SIDE) * (1.0 / BASE) + 0.5 / BASE)
    kz = b - ky * BASE

    def table_step(index, _):
        lanes = pl.ds(pl.multiple_of(index * CHUNK, CHUNK), CHUNK)
        xyz = coords_ref[:, lanes]
        ta = cos_sin(ka * xyz[0:1])
        ta_ref[0:top, lanes] = ta[0].astype(BF16)
        ta_ref[top:a, lanes] = ta[1].astype(BF16)
        tb = cos_sin(ky * xyz[1:2] + kz * xyz[2:3])
        tb_ref[0:top, lanes] = tb[0]
        tb_ref[top:a, lanes] = tb[1]
        return 0

    lax.fori_loop(0, coords_ref.shape[1] // CHUNK, table_step, 0)
    ta = ta_ref[...]
    h = h_ref[...]
    for first, size in groups_of(pairs):
        cs, ss = zip(*[phase_rows(ta, tb_ref, first + i, pairs) for i in range(size)])
        rows = slice(first * a, (first + size) * a)
        c = lax.dot_general(jnp.concatenate(cs, 0), h, NT, preferred_element_type=F32)
        s = lax.dot_general(jnp.concatenate(ss, 0), h, NT, preferred_element_type=F32)
        out_ref[rows, :] = jnp.concatenate([c, s], 1).astype(BF16)
    c = lax.dot_general(tb_ref[...].astype(BF16), h, NT, preferred_element_type=F32)
    out_ref[pairs * a : (pairs + 1) * a, :] = jnp.concatenate([c, jnp.zeros_like(c)], 1).astype(BF16)
    rest = out_ref.shape[0] - (pairs + 1) * a
    if rest:
        out_ref[(pairs + 1) * a :, :] = jnp.zeros((rest, out_ref.shape[1]), BF16)
    for copy in copies:
        copy.wait()


def exchange_kernel(
    scale_x,
    scale,
    a,
    idx_ref,
    live_ref,
    factor_ref,
    p_ref,
    q_ref,
    same_ref,
    cross_ref,
    own_ref,
    near_ref,
    hm_ref,
    out_ref,
    msg_ref,
    inbox,
    sends,
    receives,
    sends2,
    receives2,
):
    here = lax.axis_index("atoms")
    peers = others("atoms")
    meet(peers)
    copies = [
        send(factor_ref.at[peer["atoms"]], inbox.at[d], sends, receives, d, peer) for d, peer in enumerate(peers)
    ]
    blocks = own_ref.shape[0]
    early = blocks // 2
    short_blocks(scale_x, 0, early, idx_ref, live_ref, own_ref, near_ref, hm_ref, msg_ref)
    for copy in copies:
        copy.wait()
    total = factor_ref[here].astype(F32)
    for d in range(len(peers)):
        total = total + inbox[d].astype(F32)
    total = total * scale
    half = a // 2
    parts = []
    for row in range(0, total.shape[0], a):
        parts += [total[row + half : row + a], total[row : row + half]]
    partner = jnp.concatenate(parts, 0)
    high = lax.Precision.HIGHEST
    mixed = jnp.dot(total, same_ref[...], precision=high, preferred_element_type=F32)
    crossed = jnp.dot(partner, cross_ref[...], precision=high, preferred_element_type=F32)
    out_ref[here] = (p_ref[...] * mixed + q_ref[...] * crossed).astype(BF16)
    copies = [
        send(out_ref.at[here], out_ref.at[here], sends2, receives2, d, peer) for d, peer in enumerate(peers)
    ]
    short_blocks(scale_x, early, blocks, idx_ref, live_ref, own_ref, near_ref, hm_ref, msg_ref)
    for copy in copies:
        copy.wait()


def finish_kernel(
    pairs,
    scale,
    count_ref,
    ta_ref,
    tb_ref,
    g_ref,
    h_ref,
    mine_ref,
    first_ref,
    second_ref,
    out_ref,
    msg_ref,
    pot_ref,
    sends,
    receives,
):
    wave = lax.axis_index("waves")
    peers = others("waves")
    count = len(peers)
    meet(peers)
    msg_ref[wave] = mine_ref[...]
    copies = [
        send(mine_ref, msg_ref.at[wave], sends, receives, d, peer) for d, peer in enumerate(peers)
    ]
    a = ta_ref.shape[0]
    ta = ta_ref[...]
    rows = tb_ref.shape[0]
    acc = lax.dot_general(
        g_ref[pairs * a : pairs * a + rows, 0:64], tb_ref[...].astype(BF16), TN, preferred_element_type=F32
    )
    for first, size in groups_of(pairs):
        cs, ss = zip(*[phase_rows(ta, tb_ref, first + i, pairs) for i in range(size)])
        g = g_ref[first * a : (first + size) * a, :]
        acc += lax.dot_general(g[:, 0:64], jnp.concatenate(cs, 0), TN, preferred_element_type=F32)
        acc += lax.dot_general(g[:, 64:128], jnp.concatenate(ss, 0), TN, preferred_element_type=F32)
    pot_ref[wave] = (acc * scale).astype(BF16)
    copies += [
        send(pot_ref.at[wave], pot_ref.at[wave], sends, receives, count + d, peer) for d, peer in enumerate(peers)
    ]
    for copy in copies:
        copy.wait()
    h = h_ref[...]
    pot = pot_ref[0].astype(F32)
    for w in range(1, pot_ref.shape[0]):
        pot = pot + pot_ref[w].astype(F32)
    msg = jnp.concatenate(
        [msg_ref[w, b] for w in range(msg_ref.shape[0]) for b in range(msg_ref.shape[1])], 1
    )
    z = jnp.concatenate([h, msg, pot.astype(BF16)], 0)
    hidden = jnp.dot(first_ref[...], z, preferred_element_type=F32)
    hidden = (hidden * jax.nn.sigmoid(hidden)).astype(BF16)
    out = h.astype(F32) + jnp.dot(second_ref[...], hidden, preferred_element_type=F32)
    atom = lax.broadcasted_iota(jnp.int32, out.shape, 1)
    out_ref[...] = jnp.where(atom < count_ref[0] * BLOCK, out, 0.0).astype(BF16)


def short_blocks(scale_x, begin, end, idx_ref, live_ref, own_ref, near_ref, hm_ref, out_ref):
    steps = idx_ref.shape[0] // BATCH

    def block_step(b, _):
        own = own_ref[b]
        cols = [jnp.broadcast_to(own[:, d : d + 1], (BLOCK, BLOCK)) for d in range(3)]

        def slot_step(step, acc):
            weights, mapped = [], []
            for u in range(BATCH):
                s = step * BATCH + u
                n = idx_ref[s, b]
                near = near_ref[n]
                total = None
                for d in (1, 2, 0):
                    diff = cols[d] - near[d : d + 1, :]
                    diff = diff - jnp.round(diff)
                    if d == 0:
                        diff = diff * scale_x
                    total = diff * diff if total is None else total + diff * diff
                weights.append(jnp.exp2(total * (-2.0 * math.log2(math.e))).astype(BF16))
                mapped.append(hm_ref[n] * live_ref[s, b].astype(BF16))
            return acc + lax.dot_general(
                jnp.concatenate(mapped, 1), jnp.concatenate(weights, 1), NT, preferred_element_type=F32
            )

        acc = lax.fori_loop(0, steps, slot_step, jnp.zeros((hm_ref.shape[1], BLOCK), F32))
        out_ref[b] = (acc * MSG_SCALE).astype(BF16)
        return 0

    lax.fori_loop(begin, end, block_step, 0)


def call(kernel, ident, shapes, specs, scratch, *args):
    return pl.pallas_call(
        kernel,
        out_shape=[jax.ShapeDtypeStruct(shape, dtype) for shape, dtype in shapes],
        in_specs=specs,
        out_specs=[VMEM] * len(shapes),
        scratch_shapes=scratch,
        compiler_params=pltpu.CompilerParams(
            vmem_limit_bytes=48 * 1024 * 1024, collective_id=ident, has_side_effects=True
        ),
    )(*args)


def coefficients(kvec, regions, pairs, padded, first, here, owned, chans):
    top = 2 * regions
    k = jnp.where(kvec[0:1] < 0, -kvec, kvec)
    code = k[1] * BASE + k[2]
    n = jnp.abs(code) - first
    onehot_a = (jnp.arange(top + 1, dtype=F32)[:, None] == k[0][None, :]).astype(BF16)
    which = jnp.arange(pairs, dtype=F32)[:, None] == n[None, :]
    up = (which & (code >= 0)[None, :]).astype(BF16)
    down = (which & (code < 0)[None, :]).astype(BF16)
    m1 = lax.dot_general(up, onehot_a, NT, preferred_element_type=F32)
    m2 = lax.dot_general(down, onehot_a, NT, preferred_element_type=F32)
    b = jnp.arange(pairs, dtype=F32) + first
    ky = jnp.floor((b + SIDE) / BASE)
    kz = b - ky * BASE
    kx = jnp.arange(top + 1, dtype=F32) / regions
    gain = GAIN_TOP / (4.0 + (kx * kx)[None, :] + (ky * ky + kz * kz)[:, None])
    p = gain * (m1 + m2)
    q = gain * (m2 - m1)
    main_p, main_q = p[:, 1:], q[:, 1:]
    a = 2 * top
    p_rows = jnp.concatenate([main_p, main_p], 1).reshape(-1)
    q_cos = jnp.concatenate([main_q, -main_q], 1).reshape(-1)
    extra = jnp.pad(p[:, 0], (0, a // 2 - pairs))
    extra = jnp.concatenate([extra, extra])
    rest = (padded - pairs - 1) * a
    p_cos = jnp.concatenate([p_rows, extra, jnp.zeros((rest,), F32)])
    p_sin = jnp.concatenate([p_rows, jnp.zeros((a + rest,), F32)])
    q_cos = jnp.pad(q_cos, (0, a + rest))
    p_cos, p_sin, q_cos = [lax.dynamic_slice_in_dim(x, here * owned, owned, 0) for x in (p_cos, p_sin, q_cos)]
    wide = lambda x, y: jnp.concatenate(
        [jnp.broadcast_to(v[:, None], (owned, chans)) for v in (x, y)], 1
    )
    return wide(p_cos, p_sin), wide(q_cos, -q_cos)


def local(
    features,
    coords,
    neighbours,
    live_slots,
    block_count,
    kvec,
    msg_weight,
    filter_weight,
    mlp_in,
    mlp_out,
):
    chans, width = features.shape
    nblocks = width // BLOCK
    regions = lax.axis_size("atoms")
    groups = lax.axis_size("waves")
    here = lax.axis_index("atoms")
    wave = lax.axis_index("waves")
    total = regions * width
    waves_total = kvec.shape[1] * groups
    top = 2 * regions
    a = 2 * top
    pairs = -(-HALF // groups)
    padded = -(-(pairs + 1) // regions) * regions
    first = (wave * pairs).astype(F32)

    h = features
    live = jnp.arange(width, dtype=jnp.int32) < block_count[0] * BLOCK
    masked = jnp.where(live[None, :], h, jnp.zeros_like(h))

    hm = jnp.dot(msg_weight[0], h, preferred_element_type=F32).astype(BF16)
    hm3 = hm.reshape(chans, nblocks, BLOCK).transpose(1, 0, 2)
    pos3 = coords.reshape(3, nblocks, BLOCK).transpose(1, 0, 2)

    copies = 4 + groups - 1
    factor, near, hm_ext, all_k, ta, tb = call(
        functools.partial(structure_kernel, pairs),
        0,
        [
            ((padded * a, 2 * chans), BF16),
            ((3 * nblocks, 3, BLOCK), F32),
            ((3 * nblocks, chans, BLOCK), BF16),
            ((groups,) + kvec.shape, F32),
            ((a, width), BF16),
            ((a, width), F32),
        ],
        [VMEM] * 5,
        [DMA((copies,)), DMA((copies,))],
        coords,
        masked,
        pos3,
        hm3,
        kvec.astype(F32),
    )
    all_k = all_k.transpose(1, 0, 2).reshape(kvec.shape[0], -1)

    source = neighbours // nblocks
    offset = (source - here) % regions
    which = jnp.where(offset == 0, 1, jnp.where(offset == 1, 2, 0))
    ext_index = which * nblocks + neighbours % nblocks
    mine = nblocks // groups
    slots = neighbours.shape[0]
    extra = -slots % BATCH
    start = wave * mine
    idx = jnp.pad(lax.dynamic_slice_in_dim(ext_index, start, mine, 1), ((0, extra), (0, 0)))
    used = jnp.pad(lax.dynamic_slice_in_dim(live_slots, start, mine, 1), ((0, extra), (0, 0))).astype(F32)
    own = lax.dynamic_slice_in_dim(pos3, start, mine, 0).transpose(0, 2, 1)
    owned = padded * a // regions
    p, q = coefficients(all_k, regions, pairs, padded, first, here, owned, chans)
    mixing = filter_weight[0]
    zero = jnp.zeros_like(mixing)
    same = jnp.block([[mixing, zero], [zero, mixing]])
    cross = jnp.block([[zero, mixing], [mixing, zero]])
    peers = regions - 1
    filtered, msg = call(
        functools.partial(exchange_kernel, float(regions), 1.0 / math.sqrt(total), a),
        1,
        [((regions, owned, 2 * chans), BF16), ((mine, chans, BLOCK), BF16)],
        [SMEM] * 2 + [VMEM] * 8,
        [pltpu.VMEM((peers, owned, 2 * chans), BF16)] + [DMA((peers,))] * 4,
        idx,
        used,
        factor.reshape(regions, owned, 2 * chans),
        p,
        q,
        same,
        cross,
        own,
        near,
        hm_ext,
    )
    peers = groups - 1
    return call(
        functools.partial(finish_kernel, pairs, 1.0 / math.sqrt(waves_total)),
        2,
        [((chans, width), BF16)],
        [SMEM] + [VMEM] * 7,
        [pltpu.VMEM((groups, mine, chans, BLOCK), BF16), pltpu.VMEM((groups, chans, width), BF16)]
        + [DMA((2 * peers,))] * 2,
        block_count,
        ta,
        tb,
        filtered.reshape(padded * a, 2 * chans),
        h,
        msg,
        mlp_in[0],
        mlp_out[0],
    )[0]


def solution(mesh):
    in_specs = (
        P(None, "atoms"),
        P(None, "atoms"),
        P(None, "atoms"),
        P(None, "atoms"),
        P("atoms"),
        P(None, "waves"),
        P(),
        P(),
        P(),
        P(),
    )
    out_specs = P(None, "atoms")
    return jax.shard_map(local, mesh=mesh, in_specs=in_specs, out_specs=out_specs, check_vma=False)
```
